32 devices in a mesh: slab: 16 (over z, y, x), blk: 2 (over core).
Axes of the slice: x: 2, y: 2, z: 4, core: 2. Of those that a mesh axis runs over, the one named last changes fastest.
Arguments:
- interior: float32 [32, 128, 512], P('slab', 'blk'), may hold values from -6 to 6
- sources: float32 [32, 128, 512], P('slab', 'blk'), may hold values from -12 to 12
- absorption: float32 [32, 128, 512], P('slab', 'blk'), may hold values from 0.1 to 4
- bem_panel: bfloat16 [8192, 16384], P('blk', 'slab'), may hold values from -0.0625 to 0.0625
- incident: bfloat16 [16384, 512], P('slab'), may hold values from -160 to 160
- node_cell: int32 [16384], P('slab'), may hold values from 0 to 255
- offset: int32 [1], replicated, may hold values from 0 to 8192, as said below
Outputs:
- relaxed: float32 [32, 128, 512], P('slab', 'blk')
- boundary_flux: float32 [8192, 512], P(('blk', 'slab'))
The draws below stay inside these ranges and needn't reach their ends.
Inputs may be any that keep to these rules, and one draw needn't show every extreme that they name: offset is a multiple of 8192; rows offset to offset + 8191 lie among the 16384 boundary nodes.
All inputs are finite; a program needn't handle non-finite values.
Results may differ from the reference program's by a relative error of at most 0.0034.
Values sent between devices are 32-bit elements; how exact they have to be, the bound alone decides.
No kernel may reach another device: no remote copies, remote signals or barrier semaphores. Data moves between devices by JAX's collectives and lax.ppermute only.
A program may use at most 64 MiB of HBM per device.

```python
import math
import jax
import jax.numpy as jnp
from jax import lax

CZ = 2
CY = 64
NX = 512
C_DEV = 512
PR = 8192
NRHS = 512
SWEEPS = 2
NZ = 32
NY = 128
NB = 16384
N_BLK = 2


def draw_incident(key, part):
    key_base, key_row, key_col = jax.random.split(key, 3)
    position = jnp.arange(NB, dtype=jnp.float32) / NB
    row_scale = 10.0 ** jax.random.uniform(key_row, (NB,), jnp.float32)
    col_scale = 10.0 ** jax.random.uniform(key_col, (NRHS,), jnp.float32)
    ramp = jnp.exp(jnp.log(3.0) * position)
    base = jnp.clip(jax.random.normal(key_base, (NB, NRHS), jnp.float32), -4.0, 4.0)
    values = 0.04 * base * (row_scale * ramp)[:, None] * col_scale[None, :]
    return values.astype(jnp.bfloat16)


def draw_offset(key, part):
    return (jax.random.randint(key, (1,), 0, NB // PR) * PR).astype(jnp.int32)


def touch_ends(result, key, smallest, largest):
    spot = [jax.random.randint(jax.random.fold_in(key, axis), (), 0, length) for axis, length in enumerate(result.shape)]
    main_axis = result.shape.index(max(result.shape))
    neighbour = spot[:main_axis] + [(spot[main_axis] + 1) % result.shape[main_axis]] + spot[main_axis + 1:]
    return result.at[tuple(spot)].set(smallest).at[tuple(neighbour)].set(largest)


def raised(values, key, source, target, blocks, factor):
    owner, partner = [(jnp.arange(values.shape[dim]) // (values.shape[dim] // blocks)).reshape([-1 if axis == dim else 1 for axis in range(values.ndim)]) for dim in (source, target)]
    chosen = jax.random.permutation(key, blocks)[partner]
    strong = (owner == chosen) | (owner == (partner + blocks // 2) % blocks)
    return jnp.where(strong, factor * values, values)


def block_scale(key, shape, pieces, least, largest):
    loudness, own = 1.0, jax.random.fold_in(key, 6)
    for dim, parts in pieces:
        heights = jnp.exp(jax.random.uniform(jax.random.fold_in(own, dim), (parts,), jnp.float32, least / len(pieces), largest / len(pieces)))
        loudness = loudness * jnp.repeat(heights, shape[dim] // parts).reshape([-1 if axis == dim else 1 for axis in range(len(shape))])
    return loudness


def gaussian(rng, shape, width, reach, cuts=(), held_as=jnp.bfloat16):
    entries = width * jax.random.normal(rng, shape, jnp.float32)
    if cuts:
        entries = entries * block_scale(rng, shape, cuts, -0.22, 0.18)
    return jnp.clip(entries, -reach, reach).astype(held_as)


def heavy_noise(key, shape, deviation, reach, cuts, heavy, kind=jnp.bfloat16):
    entries = deviation * jax.random.normal(key, shape, jnp.float32)
    if cuts:
        entries = entries * block_scale(key, shape, cuts, -0.22, 0.18)
    return jnp.clip(raised(entries, jax.random.fold_in(key, 3), *heavy), -reach, reach).astype(kind)


def setup_inputs(seed: int = 0) -> dict:
    key_list = jax.random.split(jax.random.key(seed), 8)
    return {
        "interior": gaussian(key_list[0], (NZ, NY, NX), 1.0, 6.0, ((0, 16), (1, 2)), jnp.float32),
        "sources": gaussian(key_list[1], (NZ, NY, NX), 2.0, 12.0, ((0, 16), (1, 2)), jnp.float32),
        "absorption": jnp.clip(jnp.exp(math.log(4.0) - 3.6888794 * jax.random.uniform(key_list[2], (NZ, NY, NX), jnp.float32) ** block_scale(key_list[2], (NZ, NY, NX), ((0, 16), (1, 2)), -0.2, 0.2)), 0.1, 4.0),
        "bem_panel": heavy_noise(key_list[3], (PR, NB), NB ** -0.5, 0.0625, ((0, 2), (1, 16)), (1, 0, 16, 2.0)),
        "incident": draw_incident(jax.random.fold_in(key_list[7], 71), 0),
        "node_cell": touch_ends(jax.random.randint(key_list[5], (NB,), 0, 2 * CZ * CY), jax.random.fold_in(key_list[5], 1), 0, (2 * CZ * CY) - 1).astype(jnp.int32),
        "offset": draw_offset(jax.random.fold_in(key_list[7], 71), 0),
    }


omega = 0.6
center_weight = 8.0 / 3.0

def stiffness(padded):
    along_x = padded[:, :, :-2] + padded[:, :, 2:]
    middle = padded[:, :, 1:-1]
    plus_mid = along_x + middle
    plane_sum = plus_mid[:, :-2] + plus_mid[:, 1:-1] + plus_mid[:, 2:]
    total_sum = plane_sum[:-2] + plane_sum[1:-1] + plane_sum[2:]
    cross_xy = along_x[:, :-2] + along_x[:, 2:]
    corner_sum = cross_xy[:-2] + cross_xy[2:]
    face_sum = along_x[1:-1, 1:-1] + middle[1:-1, :-2] + middle[1:-1, 2:] + middle[:-2, 1:-1] + middle[2:, 1:-1]
    center = middle[1:-1, 1:-1]
    edge_sum = total_sum - center - face_sum - corner_sum
    return center_weight * center - edge_sum / 6.0 - corner_sum / 12.0

def sweep_once(padded, sources, absorption):
    center = padded[1:-1, 1:-1, 1:-1]
    applied = stiffness(padded) + absorption * center
    return center + omega * (sources - applied) / (center_weight + absorption)

def reference(interior, sources, absorption, bem_panel, incident, node_cell, offset):
    current = interior
    for sweep_idx in range(SWEEPS):
        current = sweep_once(jnp.pad(current, 1), sources, absorption)
    nodes = jnp.arange(NB, dtype=jnp.int32)
    block = nodes // C_DEV
    zpos = block // N_BLK * CZ + node_cell // (2 * CY)
    ypos = block % N_BLK * CY + node_cell // 2 % CY
    xpos = node_cell % 2 * (NX - 1)
    trace = interior[zpos, ypos, xpos]
    fields = (incident.astype(jnp.float32) + trace[:, None]).astype(jnp.bfloat16)
    wide = fields.astype(jnp.float32)
    norms = jnp.sqrt(lax.optimization_barrier(jnp.sum(wide * wide, axis=0)) / NB + 1e-06)
    jump = lax.dynamic_slice_in_dim(wide, offset[0].astype(jnp.int32), PR, 0)
    product = jnp.dot(bem_panel, fields, preferred_element_type=jnp.float32) + 0.5 * jump
    return (current, product / norms[None, :])
```

```python
import jax
import jax.numpy as jnp
from jax import lax
from jax.sharding import PartitionSpec as P

SWEEPS = 2

omega = 0.6
center_weight = 8.0 / 3.0

PIECES = ((8, (0, 2, 1)), (10, (2, 1, 0)), (10, (1, 2, 0)), (4, (0, 1, 2)))


def slab_dims(count):
    bits = count.bit_length() - 1
    if count != 1 << bits or bits > 6:
        return None
    dims = [1, 1, 1]
    for bit in range(bits):
        dims[bit % 3] *= 2
    return tuple(dims)


def strides_of(dims):
    return (dims[1] * dims[2], dims[2], 1)


def pairs_along(dims, axis, hops):
    stride = strides_of(dims)[axis]
    count = dims[0] * dims[1] * dims[2]
    found = []
    for source in range(count):
        here = source // stride % dims[axis]
        for begin, end in hops:
            if begin == here:
                found.append((source, source + (end - begin) * stride))
    return found


def pick(array, index, axis):
    return lax.dynamic_index_in_dim(array, index, axis, keepdims=False)


def reduce_line(data, dims, axis, dim_pos, place):
    size = dims[axis]
    if size == 1:
        return jnp.squeeze(data, dim_pos)
    swap = [(0, 1), (1, 0)]
    if size == 2:
        send = pick(data, 1 - place, dim_pos)
        got = lax.ppermute(send, "slab", pairs_along(dims, axis, swap))
        return pick(data, place, dim_pos) + got
    shape = data.shape
    data = data.reshape(shape[:dim_pos] + (2, 2) + shape[dim_pos + 1 :])
    side = place // 2
    near = pick(data, side, dim_pos)
    far = pick(data, 1 - side, dim_pos)
    got = lax.ppermute(far, "slab", pairs_along(dims, axis, [(0, 1), (3, 2)]))
    got = lax.ppermute(far + got, "slab", pairs_along(dims, axis, [(1, 2), (2, 1)]))
    near = near + got
    send = pick(near, 1 - place % 2, dim_pos)
    got = lax.ppermute(send, "slab", pairs_along(dims, axis, swap + [(2, 3), (3, 2)]))
    return pick(near, place % 2, dim_pos) + got


def reduce_scatter(product, dims):
    index = lax.axis_index("slab")
    strides = strides_of(dims)
    places = [index // strides[axis] % dims[axis] for axis in range(3)]
    rows = product.shape[0] // (dims[0] * dims[1] * dims[2])
    chunks = product.reshape(dims + (rows, product.shape[1]))
    parts = []
    first = 0
    done = 0
    for share, order in PIECES:
        done += share
        last = rows * done // 32
        data = chunks[:, :, :, first:last]
        left = [0, 1, 2]
        for axis in order:
            data = reduce_line(data, dims, axis, left.index(axis), places[axis])
            left.remove(axis)
        parts.append(data)
        first = last
    return jnp.concatenate(parts, axis=0)


def sum_slabs(values, count):
    step = 1
    while step < count:
        values = values + lax.ppermute(values, "slab", [(i, i ^ step) for i in range(count)])
        step *= 2
    return values


def padded_2(cells, sides, width):
    for axis, dim in sides:
        count = lax.axis_size(axis)
        head = lax.slice_in_dim(cells, 0, width, axis=dim)
        tail = lax.slice_in_dim(cells, cells.shape[dim] - width, cells.shape[dim], axis=dim)
        if count == 2:
            first = lax.axis_index(axis) == 0
            got = lax.ppermute(jnp.where(first, tail, head), axis, [(0, 1), (1, 0)])
            before, after = jnp.where(first, 0.0, got), jnp.where(first, got, 0.0)
        else:
            ends = count - 1
            before = lax.ppermute(tail, axis, [(i, i + 1) for i in range(ends)])
            after = lax.ppermute(head, axis, [(i + 1, i) for i in range(ends)])
        cells = jnp.concatenate([before, cells, after], axis=dim)
    return cells


def stiffness(padded):
    along_x = padded[:, :, :-2] + padded[:, :, 2:]
    middle = padded[:, :, 1:-1]
    plus_mid = along_x + middle
    plane_sum = plus_mid[:, :-2] + plus_mid[:, 1:-1] + plus_mid[:, 2:]
    total_sum = plane_sum[:-2] + plane_sum[1:-1] + plane_sum[2:]
    cross_xy = along_x[:, :-2] + along_x[:, 2:]
    corner_sum = cross_xy[:-2] + cross_xy[2:]
    face_sum = (
        along_x[1:-1, 1:-1]
        + middle[1:-1, :-2]
        + middle[1:-1, 2:]
        + middle[:-2, 1:-1]
        + middle[2:, 1:-1]
    )
    center = middle[1:-1, 1:-1]
    edge_sum = total_sum - center - face_sum - corner_sum
    return center_weight * center - edge_sum / 6.0 - corner_sum / 12.0


def sweep_once(padded, sources, absorption):
    center = padded[1:-1, 1:-1, 1:-1]
    applied = stiffness(padded) + absorption * center
    return center + omega * (sources - applied) / (center_weight + absorption)


def pad_x(values):
    return jnp.pad(values, ((0, 0), (0, 0), (1, 1)))


def per_device(interior, sources, absorption, bem_panel, incident, node_cell, offset):
    depth_z, depth_y, width_x = interior.shape
    slab_count = lax.axis_size("slab")
    blk_count = lax.axis_size("blk")
    slab_cols = incident.shape[0]
    panel_rows = bem_panel.shape[0]
    own_count = slab_cols // blk_count

    x_faces = jnp.stack([interior[:, :, 0], interior[:, :, width_x - 1]], axis=-1).reshape(-1)
    own_cells = lax.dynamic_slice_in_dim(node_cell, lax.axis_index("blk") * own_count, own_count, 0)
    own_trace = jnp.take(x_faces, own_cells, axis=0)
    trace = lax.all_gather(own_trace, "blk", axis=0, tiled=True)
    fields = (incident.astype(jnp.float32) + trace[:, None]).astype(jnp.bfloat16)
    wide = fields.astype(jnp.float32)
    node_total = slab_cols * slab_count

    common = min(panel_rows, slab_cols)
    shift = offset[0] + lax.axis_index("blk") * panel_rows - lax.axis_index("slab") * slab_cols
    row_at = jnp.clip(-shift, 0, panel_rows - common)
    node_at = jnp.clip(shift, 0, slab_cols - common)
    meets = (shift + panel_rows > 0) & (shift < slab_cols)
    jump = jnp.where(meets, 0.5, 0.0) * lax.dynamic_slice_in_dim(wide, node_at, common, 0)
    product = jnp.dot(bem_panel, fields, preferred_element_type=jnp.float32)
    old = lax.dynamic_slice_in_dim(product, row_at, common, 0)
    product = lax.dynamic_update_slice_in_dim(product, old + jump, row_at, 0)

    owned = reduce_scatter(product, slab_dims(slab_count))
    squares = sum_slabs(jnp.sum(wide * wide, axis=0, keepdims=True), slab_count)
    norms = jnp.sqrt(squares / node_total + 1e-06)

    current = interior
    for sweep_idx in range(SWEEPS):
        padded = padded_2(current, (("slab", 0), ("blk", 1)), 1)
        current = sweep_once(pad_x(padded), sources, absorption)
    return (current, owned / norms)


def solution(mesh):
    in_specs = (
        P("slab", "blk", None),
        P("slab", "blk", None),
        P("slab", "blk", None),
        P("blk", "slab"),
        P("slab", None),
        P("slab"),
        P(),
    )
    out_specs = (P("slab", "blk", None), P(("blk", "slab"), None))
    return jax.shard_map(
        per_device, mesh=mesh, in_specs=in_specs, out_specs=out_specs, check_vma=False
    )
```

```python
import functools

import jax
import jax.numpy as jnp
from jax import lax
from jax.experimental import pallas as pl
from jax.experimental.pallas import tpu as pltpu
from jax.sharding import PartitionSpec as P

SWEEPS = 2

omega = 0.6
center_weight = 8.0 / 3.0
LANES = 128
ROW_UNIT = 16
TILE = 8
LIMIT = 24 * 2**20

PIECES = ((2, (0, 2, 1)), (4, (1, 2, 0)), (4, (2, 0, 1)), (3, (0, 1, 2)), (3, (1, 2, 0)))
ARRIVALS = (0, 0, 1, 3, 2, 0, 1, 0, 4, 2, 0, 3, 1, 4, 2, 3, 4, 1, 3, 2, 4, 3, 1, 2, 4)
EARLY = 3
CARRIER = 0


def slab_dims(count):
    bits = count.bit_length() - 1
    if count != 1 << bits or bits > 6:
        return None
    dims = [1, 1, 1]
    for bit in range(bits):
        dims[bit % 3] *= 2
    return tuple(dims)


def strides_of(dims):
    return (dims[1] * dims[2], dims[2], 1)


def pairs_along(dims, axis, hops):
    stride = strides_of(dims)[axis]
    count = dims[0] * dims[1] * dims[2]
    found = []
    for source in range(count):
        here = source // stride % dims[axis]
        for begin, end in hops:
            if begin == here:
                found.append((source, source + (end - begin) * stride))
    return found


def others_of(axis):
    return [other for other in range(3) if other != axis]


class Piece:
    def __init__(self, first, rows, order, dims, extra):
        self.first, self.rows, self.order, self.dims, self.extra = first, rows, order, dims, extra
        self.steps = []
        left = [0, 1, 2]
        for axis in order:
            count = 1
            for other in left:
                count *= dims[other] if other != axis else 1
            if dims[axis] == 2:
                self.steps.append(("swap", axis, tuple(left), count))
            elif dims[axis] == 4:
                for kind in ("outer", "inner", "swap4"):
                    self.steps.append((kind, axis, tuple(left), count))
            left.remove(axis)

    def height(self):
        return self.rows + self.extra

    def halves(self, number, places):
        _, axis, left, _ = self.steps[number]
        spans = [self.dims[other] for other in left]
        at = left.index(axis)
        inner = 1
        for span in spans[at + 1 :]:
            inner *= span
        outer = 1
        for span in spans[:at]:
            outer *= span
        size, place = spans[at], places[axis]
        if size == 2:
            sent, kept = [1 - place], [place]
        else:
            side = place // 2
            sent, kept = [2 - 2 * side, 3 - 2 * side], [2 * side, 2 * side + 1]
        return [
            [i * (size * inner) + block * inner + j for i in range(outer) for block in half for j in range(inner)]
            for half in (sent, kept)
        ]

    def halves_of_two(self, number, places):
        _, axis, left, _ = self.steps[number]
        inner = 1
        for other in left[left.index(axis) + 1 :]:
            inner *= self.dims[other]
        outer = self.steps[number][3] // inner
        own = lax.rem(jnp.asarray(places[axis], jnp.int32), 2)
        return [
            [i * (2 * inner) + at * inner + j for i in range(outer) for j in range(inner)]
            for at in (1 - own, own)
        ]

    def window(self, which, places):
        axis = self.order[0]
        place, index = places[axis], [slice(None)] * 3
        if self.dims[axis] == 2:
            index[axis] = 1 - place if which == 0 else place
        else:
            side = place // 2
            index[axis] = pl.ds(2 - 2 * side if which == 0 else 2 * side, 2)
        return tuple(index) + (pl.ds(self.first, self.rows), slice(None))

    def window_shape(self):
        axis = self.order[0]
        spans = [self.dims[other] // 2 if other == axis else self.dims[other] for other in range(3)]
        if self.dims[axis] == 2:
            del spans[axis]
        return tuple(spans) + (self.rows,)

    def pairs(self, number):
        kind, axis, _, _ = self.steps[number]
        hops = {
            "swap": [(0, 1), (1, 0)],
            "outer": [(0, 1), (3, 2)],
            "inner": [(1, 2), (2, 1)],
            "swap4": [(0, 1), (1, 0), (2, 3), (3, 2)],
        }[kind]
        return pairs_along(self.dims, axis, hops)


def places_of(slab, dims):
    strides = strides_of(dims)
    return [lax.rem(lax.div(slab, strides[axis]), dims[axis]) for axis in range(3)]


def panel_copies(pieces, which, panel, panel_bufs, sems):
    places = places_of(lax.axis_index("slab"), pieces[0].dims)
    jobs = []
    for number, piece in enumerate(pieces):
        copy = pltpu.make_async_copy(
            panel.at[piece.window(which, places)], panel_bufs[number], sems.at[number]
        )
        copy.start()
        jobs.append((piece, piece.halves(0, places)[which], copy, panel_bufs[number]))
    return jobs


def multiply(jobs, shift, chunk_rows, fields, squares, outs):
    node_count, width = fields.shape
    for (piece, chunks, copy, panel_buf), out in zip(jobs, outs):
        copy.wait()
        rows = piece.rows
        lhs = panel_buf[...].reshape(len(chunks) * rows, node_count)
        product = jnp.dot(lhs, fields[...], preferred_element_type=jnp.float32)
        for block, chunk in enumerate(chunks):
            out[block, 0:rows, :] = product[block * rows : (block + 1) * rows]
            node = shift + chunk * chunk_rows

            @pl.when((node >= 0) & (node < node_count))
            def _(block=block, node=node):
                at = pl.multiple_of(node + piece.first, ROW_UNIT)
                jump = fields[pl.ds(at, rows), :].astype(jnp.float32)
                out[block, 0:rows, :] += 0.5 * jump

            if piece.extra:
                row = lax.broadcasted_iota(jnp.int32, (TILE, width), 0)
                out[block, rows : rows + TILE, :] = jnp.where(row == 0, squares[...], 0.0)


def make_fields(blk, interiors, cells, incident, fields, squares):
    tables = []
    for block in interiors:
        depth_z, depth_y, width = block.shape
        flat_left = block[:, :, :LANES].reshape(depth_z * depth_y, LANES)
        flat_right = block[:, :, width - LANES :].reshape(depth_z * depth_y, LANES)
        tables.append((flat_left.T[0:1, :], flat_right.T[LANES - 1 : LANES, :]))
    node_count = incident.shape[0]
    per_block = node_count // (2 if len(interiors) == 2 else len(interiors))
    across = cells[...].T
    lane = lax.broadcasted_iota(jnp.int32, (LANES, tables[0][0].shape[1]), 1)
    total = jnp.zeros((8, incident.shape[1]), jnp.float32)
    for part in range(node_count // LANES):
        owner = part * LANES // per_block
        if len(interiors) == 2:
            mine = blk == owner
            left = jnp.where(mine, tables[0][0], tables[1][0])
            right = jnp.where(mine, tables[0][1], tables[1][1])
        else:
            left, right = tables[owner]
        cell = across[:, part : part + 1]
        column = cell >> 1
        value = jnp.where((cell & 1) == 1, right, left)
        trace = jnp.sum(jnp.where(lane == column, value, 0.0), axis=1, keepdims=True)
        rows = pl.ds(part * LANES, LANES)
        field = (incident[rows, :].astype(jnp.float32) + trace).astype(jnp.bfloat16)
        fields[rows, :] = field
        wide = field.astype(jnp.float32)
        total = total + jnp.sum((wide * wide).reshape(LANES // 8, 8, wide.shape[1]), axis=0)
    squares[...] = jnp.sum(total, axis=0, keepdims=True)


def shift_of(offset, panel_rows, node_count):
    return (
        offset[0] + lax.axis_index("blk") * panel_rows - lax.axis_index("slab") * node_count
    )


def first_kernel(pieces, blocks, offset, *refs):
    interiors, refs = refs[:blocks], refs[blocks:]
    cells, incident, panel, fields, squares = refs[:5]
    count = len(pieces)
    outs, refs = refs[5 : 5 + count], refs[5 + count :]
    panel_bufs, refs = refs[:count], refs[count:]
    interior_bufs, refs = refs[:blocks], refs[blocks:]
    cells_buf, incident_buf, sems, in_sems = refs
    copies = []
    sources = list(interiors) + [cells, incident]
    targets = list(interior_bufs) + [cells_buf, incident_buf]
    for number, (source, target) in enumerate(zip(sources, targets)):
        copy = pltpu.make_async_copy(source, target, in_sems.at[number])
        copy.start()
        copies.append(copy)
    jobs = panel_copies(pieces, 0, panel, panel_bufs, sems)
    for copy in copies:
        copy.wait()
    make_fields(lax.axis_index("blk"), interior_bufs, cells_buf, incident_buf, fields, squares)
    chunk_rows = panel.shape[3]
    shift = shift_of(offset, chunk_rows * lax.axis_size("slab"), incident.shape[0])
    multiply(jobs, shift, chunk_rows, fields, squares, outs)


def later_kernel(pieces, which, offset, fields, squares, panel, token, *refs):
    count = len(pieces)
    outs, panel_bufs = refs[:count], refs[count : 2 * count]
    sems = refs[2 * count]
    jobs = panel_copies(pieces, which, panel, panel_bufs, sems)
    chunk_rows = panel.shape[3]
    shift = shift_of(offset, chunk_rows * lax.axis_size("slab"), fields.shape[0])
    multiply(jobs, shift, chunk_rows, fields, squares, outs)


def piece_scratch(pieces, depth):
    return [
        pltpu.VMEM(piece.window_shape() + (depth,), jnp.bfloat16) for piece in pieces
    ], pltpu.SemaphoreType.DMA((len(pieces),))


def piece_shapes(pieces, width):
    return [
        pltpu.VMEM((len(piece.halves(0, [0, 0, 0])[0]), piece.height(), width), jnp.float32)
        for piece in pieces
    ]


def piece_cost(pieces, depth, width):
    rows = sum(piece.rows * len(piece.halves(0, [0, 0, 0])[0]) for piece in pieces)
    return pl.CostEstimate(
        flops=2 * rows * depth * width, bytes_accessed=2 * rows * depth, transcendentals=0
    )


IN_HBM = pl.BlockSpec(memory_space=pltpu.HBM)
ANYWHERE = pl.BlockSpec(memory_space=pl.ANY)
IN_VMEM = pl.BlockSpec(memory_space=pltpu.VMEM)
IN_SMEM = pl.BlockSpec(memory_space=pltpu.SMEM)
PARAMS = pltpu.CompilerParams(vmem_limit_bytes=LIMIT)


def in_hbm(array):
    return pltpu.with_memory_space_constraint(array, pltpu.HBM)


def first_products(pieces, offset, interiors, cells, incident, panel):
    depth, width = incident.shape
    bufs, sems = piece_scratch(pieces, depth)
    return pl.pallas_call(
        functools.partial(first_kernel, pieces, len(interiors)),
        in_specs=[IN_SMEM] + [ANYWHERE] * len(interiors) + [IN_HBM] * 3,
        out_specs=[IN_VMEM] * (2 + len(pieces)),
        out_shape=[pltpu.VMEM(incident.shape, jnp.bfloat16), pltpu.VMEM((1, width), jnp.float32)]
        + piece_shapes(pieces, width),
        scratch_shapes=bufs
        + [pltpu.VMEM(block.shape, block.dtype) for block in interiors]
        + [pltpu.VMEM(cells.shape, cells.dtype), pltpu.VMEM(incident.shape, incident.dtype)]
        + [sems, pltpu.SemaphoreType.DMA((len(interiors) + 2,))],
        compiler_params=PARAMS,
        cost_estimate=piece_cost(pieces, depth, width),
        name="fields_and_first_rows",
    )(offset, in_hbm(interiors[0]), *interiors[1:], in_hbm(cells), in_hbm(incident), in_hbm(panel))


def later_products(pieces, which, offset, fields, squares, panel, token):
    depth, width = fields.shape
    bufs, sems = piece_scratch(pieces, depth)
    return pl.pallas_call(
        functools.partial(later_kernel, pieces, which),
        in_specs=[IN_SMEM, IN_VMEM, IN_VMEM, IN_HBM, ANYWHERE],
        out_specs=[IN_VMEM] * len(pieces),
        out_shape=piece_shapes(pieces, width),
        scratch_shapes=bufs + [sems],
        compiler_params=PARAMS,
        cost_estimate=piece_cost(pieces, depth, width),
        name="kept_rows" if which else "sent_rows",
    )(offset, fields, squares, in_hbm(panel), token)


def arrival_kernel(pick_blocks, dims, got, base, token, *outs):
    picked = pick_blocks(places_of(lax.axis_index("slab"), dims))
    for blocks, out in zip(picked, outs):
        for number, block in enumerate(blocks):
            out[number] = got[block] + base[block]


def add_arrival(pick_blocks, dims, got, base, token, name):
    shapes = [
        pltpu.VMEM((len(blocks),) + base.shape[1:], jnp.float32) for blocks in pick_blocks([0, 0, 0])
    ]
    return pl.pallas_call(
        functools.partial(arrival_kernel, pick_blocks, dims),
        in_specs=[IN_VMEM, IN_VMEM, ANYWHERE],
        out_specs=[IN_VMEM] * len(shapes),
        out_shape=shapes,
        compiler_params=PARAMS,
        cost_estimate=pl.CostEstimate(flops=base.size, bytes_accessed=4 * base.size, transcendentals=0),
        name=name,
    )(got, base, token)


class Course:
    def __init__(self, piece, number, far, near):
        self.piece, self.number = piece, number
        self.step, self.near, self.sent = 0, near, far
        self.done = None
        self.start()

    def start(self):
        self.got = lax.ppermute(self.sent, "slab", self.piece.pairs(self.step))

    def arrive(self, token):
        piece, step = self.piece, self.step
        kind, axis, _, count = piece.steps[step]
        last = step + 1 == len(piece.steps)
        base = self.near
        if kind == "outer":
            base = self.sent
            pick_blocks = lambda places: [list(range(2 * count))]
        elif kind == "inner":
            pick_blocks = lambda places: piece.halves_of_two(step, places)
        elif last:
            pick_blocks = lambda places: [[0]]
        else:
            pick_blocks = lambda places: piece.halves(step + 1, places)
        outs = add_arrival(
            pick_blocks, piece.dims, self.got, base, token, f"arrival_{self.number}_{step}"
        )
        if last:
            self.done = outs[0]
        else:
            if kind != "outer":
                self.near = outs[1]
            self.sent = outs[0]
            self.step += 1
            self.start()
        return outs[0]


def finish_kernel(node_total, carrier, rows, *refs):
    parts, out = refs[:-1], refs[-1]
    squares = parts[carrier][0, rows[carrier] : rows[carrier] + 1, :]
    norms = jnp.sqrt(squares / node_total + 1e-06)
    first = 0
    for part, height in zip(parts, rows):
        out[first : first + height, :] = part[0, :height, :] / norms
        first += height


def edge_rows(cells, other):
    count = lax.axis_size("blk")
    head, tail = cells[:, :1], cells[:, -1:]
    if count == 2:
        first = lax.axis_index("blk") == 0
        if other is None:
            got = lax.ppermute(jnp.where(first, tail, head), "blk", [(0, 1), (1, 0)])
        else:
            got = jnp.where(first, other[:, :1], other[:, -1:])
        return jnp.where(first, 0.0, got), jnp.where(first, got, 0.0)
    ends = count - 1
    return (
        lax.ppermute(tail, "blk", [(i, i + 1) for i in range(ends)]),
        lax.ppermute(head, "blk", [(i + 1, i) for i in range(ends)]),
    )


def with_halo(cells, other):
    before, after = edge_rows(cells, other)
    cells = jnp.concatenate([before, cells, after], axis=1)
    ends = lax.axis_size("slab") - 1
    below = lax.ppermute(cells[-1:], "slab", [(i, i + 1) for i in range(ends)])
    above = lax.ppermute(cells[:1], "slab", [(i + 1, i) for i in range(ends)])
    return jnp.concatenate([below, cells, above], axis=0)


def stiffness(padded):
    along_x = padded[:, :, :-2] + padded[:, :, 2:]
    middle = padded[:, :, 1:-1]
    plus_mid = along_x + middle
    plane_sum = plus_mid[:, :-2] + plus_mid[:, 1:-1] + plus_mid[:, 2:]
    total_sum = plane_sum[:-2] + plane_sum[1:-1] + plane_sum[2:]
    cross_xy = along_x[:, :-2] + along_x[:, 2:]
    corner_sum = cross_xy[:-2] + cross_xy[2:]
    face_sum = (
        along_x[1:-1, 1:-1]
        + middle[1:-1, :-2]
        + middle[1:-1, 2:]
        + middle[:-2, 1:-1]
        + middle[2:, 1:-1]
    )
    center = middle[1:-1, 1:-1]
    edge_sum = total_sum - center - face_sum - corner_sum
    return center_weight * center - edge_sum / 6.0 - corner_sum / 12.0


def sweep_once(padded, sources, absorption):
    center = padded[1:-1, 1:-1, 1:-1]
    applied = stiffness(padded) + absorption * center
    return center + omega * (sources - applied) / (center_weight + absorption)


def pad_x(values):
    return jnp.pad(values, ((0, 0), (0, 0), (1, 1)))


def per_device(interior, sources, absorption, bem_panel, incident, node_cell, offset):
    slab_count = lax.axis_size("slab")
    blk_count = lax.axis_size("blk")
    slab_cols, width = incident.shape
    panel_rows = bem_panel.shape[0]
    node_total = slab_cols * slab_count
    chunk_rows = panel_rows // slab_count
    dims = slab_dims(slab_count)

    if blk_count == 2:
        other = lax.ppermute(interior, "blk", [(0, 1), (1, 0)])
        interiors = [interior, other]
    else:
        other = None
        gathered = lax.all_gather(interior, "blk", axis=0)
        interiors = [gathered[i] for i in range(blk_count)]

    units, first, done = chunk_rows // ROW_UNIT, 0, 0
    spans = []
    for share, order in PIECES:
        done += share
        last = (units * done // 16) * ROW_UNIT
        if last > first:
            spans.append((first, last - first, order))
        first = last
    carrier = min(CARRIER, len(spans) - 1)
    pieces = [
        Piece(at, rows, order, dims, TILE if number == carrier else 0)
        for number, (at, rows, order) in enumerate(spans)
    ]
    cells = node_cell.reshape(slab_cols // LANES, LANES)

    panel = bem_panel.reshape(dims + (chunk_rows, slab_cols))
    early, late = pieces[:EARLY], pieces[EARLY:]
    fields, squares, *far = first_products(early, offset, interiors, cells, incident, panel)
    token = far[0]
    if late:
        more = later_products(late, 0, offset, fields, squares, panel, token)
        far, token = list(far) + list(more), more[0]
    near = later_products(pieces, 1, offset, fields, squares, panel, token)
    token = near[0]
    courses = [
        Course(piece, number, sent, kept)
        for number, (piece, sent, kept) in enumerate(zip(pieces, far, near))
    ]
    steps = sum(len(piece.steps) for piece in pieces)
    arrivals = ARRIVALS if steps == len(ARRIVALS) else list(range(len(pieces))) * steps
    for number in arrivals:
        if courses[number].done is None:
            token = courses[number].arrive(token)
    owned = pl.pallas_call(
        functools.partial(finish_kernel, node_total, carrier, [piece.rows for piece in pieces]),
        in_specs=[IN_VMEM] * len(pieces),
        out_specs=IN_VMEM,
        out_shape=jax.ShapeDtypeStruct((chunk_rows, width), jnp.float32),
        compiler_params=PARAMS,
        name="divide_by_norms",
    )(*[course.done for course in courses])

    current = interior
    for sweep_idx in range(SWEEPS):
        padded = with_halo(current, other if sweep_idx == 0 else None)
        current = sweep_once(pad_x(padded), sources, absorption)
    return (current, owned)


def solution(mesh):
    in_specs = (
        P("slab", "blk", None),
        P("slab", "blk", None),
        P("slab", "blk", None),
        P("blk", "slab"),
        P("slab", None),
        P("slab"),
        P(),
    )
    out_specs = (P("slab", "blk", None), P(("blk", "slab"), None))
    return jax.shard_map(
        per_device, mesh=mesh, in_specs=in_specs, out_specs=out_specs, check_vma=False
    )
```

```python
import functools

import jax
import jax.numpy as jnp
from jax import lax
from jax.experimental import pallas as pl
from jax.experimental.pallas import tpu as pltpu
from jax.sharding import PartitionSpec as P

SWEEPS = 2

omega = 0.6
center_weight = 8.0 / 3.0
LANES = 128
ROW_UNIT = 16
TILE = 8
LIMIT = 24 * 2**20

PIECES = ((4, (0, 1, 3, 2)), (4, (1, 0, 2, 3)), (6, (2, 1, 0, 3)), (2, (0, 2, 1, 3)))
EARLY = 3
CARRIER = 1
EVENTS = "abFN0d132031023103c212"


def bit_of(slab, bit):
    return (slab >> bit) & 1


class Piece:
    def __init__(self, first, rows, order, extra):
        self.first, self.rows, self.order, self.extra = first, rows, order, extra
        self.bits = len(order)

    def height(self):
        return self.rows + self.extra

    def halves(self, step, slab):
        left = [bit for bit in range(self.bits) if bit not in self.order[:step]]
        inner = 1 << left.index(self.order[step])
        outer = (1 << len(left)) // (2 * inner)
        own = bit_of(slab, self.order[step])
        return [
            [i * (2 * inner) + half * inner + j for i in range(outer) for j in range(inner)]
            for half in (1 - own, own)
        ]

    def window(self, which, slab):
        index = [slice(None)] * self.bits
        own = bit_of(slab, self.order[0])
        index[self.bits - 1 - self.order[0]] = own if which else 1 - own
        return tuple(index) + (pl.ds(self.first, self.rows), slice(None))

    def window_shape(self):
        return (2,) * (self.bits - 1) + (self.rows,)

    def pairs(self, step):
        return [(i, i ^ (1 << self.order[step])) for i in range(1 << self.bits)]


def panel_copies(jobs, panel, panel_bufs, sems):
    slab = lax.axis_index("slab")
    started = []
    for number, (piece, which) in enumerate(jobs):
        copy = pltpu.make_async_copy(
            panel.at[piece.window(which, slab)], panel_bufs[number], sems.at[number]
        )
        copy.start()
        started.append((piece, piece.halves(0, slab)[which], copy, panel_bufs[number]))
    return started


def multiply(jobs, shift, chunk_rows, fields, squares, outs):
    node_count, width = fields.shape
    for (piece, chunks, copy, panel_buf), out in zip(jobs, outs):
        copy.wait()
        rows = piece.rows
        lhs = panel_buf[...].reshape(len(chunks) * rows, node_count)
        product = jnp.dot(lhs, fields[...], preferred_element_type=jnp.float32)
        for block, chunk in enumerate(chunks):
            out[block, 0:rows, :] = product[block * rows : (block + 1) * rows]
            node = shift + chunk * chunk_rows

            @pl.when((node >= 0) & (node < node_count))
            def _(block=block, node=node):
                at = pl.multiple_of(node + piece.first, ROW_UNIT)
                jump = fields[pl.ds(at, rows), :].astype(jnp.float32)
                out[block, 0:rows, :] += 0.5 * jump

            if piece.extra:
                row = lax.broadcasted_iota(jnp.int32, (TILE, width), 0)
                out[block, rows : rows + TILE, :] = jnp.where(row == 0, squares[...], 0.0)


def make_fields(blk, interiors, cells, incident, fields, squares):
    tables = []
    for block in interiors:
        depth_z, depth_y, width = block.shape
        flat_left = block[:, :, :LANES].reshape(depth_z * depth_y, LANES)
        flat_right = block[:, :, width - LANES :].reshape(depth_z * depth_y, LANES)
        tables.append((flat_left.T[0:1, :], flat_right.T[LANES - 1 : LANES, :]))
    node_count = incident.shape[0]
    per_block = node_count // (2 if len(interiors) == 2 else len(interiors))
    across = cells[...].T
    lane = lax.broadcasted_iota(jnp.int32, (LANES, tables[0][0].shape[1]), 1)
    total = jnp.zeros((8, incident.shape[1]), jnp.float32)
    for part in range(node_count // LANES):
        owner = part * LANES // per_block
        if len(interiors) == 2:
            mine = blk == owner
            left = jnp.where(mine, tables[0][0], tables[1][0])
            right = jnp.where(mine, tables[0][1], tables[1][1])
        else:
            left, right = tables[owner]
        cell = across[:, part : part + 1]
        column = cell >> 1
        value = jnp.where((cell & 1) == 1, right, left)
        trace = jnp.sum(jnp.where(lane == column, value, 0.0), axis=1, keepdims=True)
        rows = pl.ds(part * LANES, LANES)
        field = (incident[rows, :].astype(jnp.float32) + trace).astype(jnp.bfloat16)
        fields[rows, :] = field
        wide = field.astype(jnp.float32)
        total = total + jnp.sum((wide * wide).reshape(LANES // 8, 8, wide.shape[1]), axis=0)
    squares[...] = jnp.sum(total, axis=0, keepdims=True)


def shift_of(offset, panel_rows, node_count):
    return (
        offset[0] + lax.axis_index("blk") * panel_rows - lax.axis_index("slab") * node_count
    )


def first_kernel(jobs, blocks, offset, *refs):
    interiors, refs = refs[:blocks], refs[blocks:]
    cells, incident, panel, fields, squares = refs[:5]
    count = len(jobs)
    outs, refs = refs[5 : 5 + count], refs[5 + count :]
    panel_bufs, refs = refs[:count], refs[count:]
    cells_buf, incident_buf, sems, in_sems = refs
    copies = []
    for number, (source, target) in enumerate(((cells, cells_buf), (incident, incident_buf))):
        copy = pltpu.make_async_copy(source, target, in_sems.at[number])
        copy.start()
        copies.append(copy)
    started = panel_copies(jobs, panel, panel_bufs, sems)
    for copy in copies:
        copy.wait()
    make_fields(lax.axis_index("blk"), interiors, cells_buf, incident_buf, fields, squares)
    chunk_rows = panel.shape[-2]
    shift = shift_of(offset, chunk_rows * lax.axis_size("slab"), incident.shape[0])
    multiply(started, shift, chunk_rows, fields, squares, outs)


def later_kernel(jobs, offset, fields, squares, panel, token, *refs):
    count = len(jobs)
    outs, panel_bufs = refs[:count], refs[count : 2 * count]
    sems = refs[2 * count]
    started = panel_copies(jobs, panel, panel_bufs, sems)
    chunk_rows = panel.shape[-2]
    shift = shift_of(offset, chunk_rows * lax.axis_size("slab"), fields.shape[0])
    multiply(started, shift, chunk_rows, fields, squares, outs)


def piece_scratch(jobs, depth):
    return [
        pltpu.VMEM(piece.window_shape() + (depth,), jnp.bfloat16) for piece, _ in jobs
    ], pltpu.SemaphoreType.DMA((len(jobs),))


def piece_shapes(jobs, width):
    return [
        pltpu.VMEM((len(piece.halves(0, 0)[0]), piece.height(), width), jnp.float32) for piece, _ in jobs
    ]


COST = pl.CostEstimate(flops=1, bytes_accessed=1, transcendentals=0)

IN_HBM = pl.BlockSpec(memory_space=pltpu.HBM)
ANYWHERE = pl.BlockSpec(memory_space=pl.ANY)
IN_VMEM = pl.BlockSpec(memory_space=pltpu.VMEM)
IN_SMEM = pl.BlockSpec(memory_space=pltpu.SMEM)
PARAMS = pltpu.CompilerParams(vmem_limit_bytes=LIMIT)


def in_hbm(array):
    return pltpu.with_memory_space_constraint(array, pltpu.HBM)


def first_products(jobs, offset, interiors, cells, incident, panel):
    depth, width = incident.shape
    bufs, sems = piece_scratch(jobs, depth)
    return pl.pallas_call(
        functools.partial(first_kernel, jobs, len(interiors)),
        in_specs=[IN_SMEM] + [IN_VMEM] * len(interiors) + [IN_HBM] * 3,
        out_specs=[IN_VMEM] * (2 + len(jobs)),
        out_shape=[pltpu.VMEM(incident.shape, jnp.bfloat16), pltpu.VMEM((1, width), jnp.float32)]
        + piece_shapes(jobs, width),
        scratch_shapes=bufs
        + [pltpu.VMEM(array.shape, array.dtype) for array in (cells, incident)]
        + [sems, pltpu.SemaphoreType.DMA((2,))],
        compiler_params=PARAMS,
        cost_estimate=COST,
        name="fields_and_first_rows",
    )(offset, *interiors, in_hbm(cells), in_hbm(incident), in_hbm(panel))


def later_products(jobs, offset, fields, squares, panel, token):
    depth, width = fields.shape
    bufs, sems = piece_scratch(jobs, depth)
    return pl.pallas_call(
        functools.partial(later_kernel, jobs),
        in_specs=[IN_SMEM, IN_VMEM, IN_VMEM, IN_HBM, ANYWHERE],
        out_specs=[IN_VMEM] * len(jobs),
        out_shape=piece_shapes(jobs, width),
        scratch_shapes=bufs + [sems],
        compiler_params=PARAMS,
        cost_estimate=COST,
        name="other_rows",
    )(offset, fields, squares, in_hbm(panel), token)


def arrival_kernel(piece, step, got, base, token, *outs):
    halves = [[0]] if step == piece.bits else piece.halves(step, lax.axis_index("slab"))
    for blocks, out in zip(halves, outs):
        for number, block in enumerate(blocks):
            out[number] = got[block] + base[block]


def add_arrival(piece, step, got, base, token, name):
    count = 1 if step == piece.bits else 2
    shape = pltpu.VMEM((max(1, base.shape[0] // 2),) + base.shape[1:], jnp.float32)
    return pl.pallas_call(
        functools.partial(arrival_kernel, piece, step),
        in_specs=[IN_VMEM, IN_VMEM, ANYWHERE],
        out_specs=[IN_VMEM] * count,
        out_shape=[shape] * count,
        compiler_params=PARAMS,
        cost_estimate=COST,
        name=name,
    )(got, base, token)


class Course:
    def __init__(self, piece, number, far):
        self.piece, self.number = piece, number
        self.step, self.near, self.done = 0, None, None
        self.send(far)

    def send(self, rows):
        self.got = lax.ppermute(rows, "slab", self.piece.pairs(self.step))

    def arrive(self, kept, token):
        base = kept if self.step == 0 else self.near
        self.step += 1
        name = f"arrival_{self.number}_{self.step}"
        outs = add_arrival(self.piece, self.step, self.got, base, token, name)
        if self.step == self.piece.bits:
            self.done = outs[0]
        else:
            self.near = outs[1]
            self.send(outs[0])
        return outs[0]


def finish_kernel(node_total, carrier, rows, *refs):
    parts, out = refs[:-1], refs[-1]
    squares = parts[carrier][0, rows[carrier] : rows[carrier] + 1, :]
    norms = jnp.sqrt(squares / node_total + 1e-06)
    first = 0
    for part, height in zip(parts, rows):
        out[first : first + height, :] = part[0, :height, :] / norms
        first += height


def ordered_kernel(count, *refs):
    for source, target in zip(refs[:count], refs[count + 1 :]):
        target[...] = source[...]


def ordered(arrays, token):
    return pl.pallas_call(
        functools.partial(ordered_kernel, len(arrays)),
        in_specs=[IN_VMEM] * len(arrays) + [ANYWHERE],
        out_specs=[IN_VMEM] * len(arrays),
        out_shape=[pltpu.VMEM(array.shape, array.dtype) for array in arrays],
        compiler_params=PARAMS,
        cost_estimate=COST,
        name="ordered",
    )(*arrays, token)


def edge_kernel(cells, before, after, *outs):
    depth, rows = cells.shape[:2]
    odd = bit_of(lax.axis_index("slab"), 0)
    for layer, lowest in zip(outs, (odd, 1 - odd)):
        at = (1 - lowest) * (depth - 1)
        layer[0, 0:rows, :] = cells[at]
        layer[0, rows : rows + 1, :] = before[at]
        layer[0, rows + 1 : rows + 2, :] = after[at]


def edge_layers(cells, before, after, token):
    shape = pltpu.VMEM((1, cells.shape[1] + 2, cells.shape[2]), jnp.float32)
    return pl.pallas_call(
        lambda cells, before, after, token, *outs: edge_kernel(cells, before, after, *outs),
        in_specs=[IN_VMEM] * 3 + [ANYWHERE],
        out_specs=[IN_VMEM] * 2,
        out_shape=[shape, shape],
        compiler_params=PARAMS,
        cost_estimate=COST,
        name="edge_layers",
    )(cells, before, after, token)


class Interior:
    def __init__(self, interior, other, sources, absorption):
        self.cells, self.sources, self.absorption = interior, sources, absorption
        self.swap = lax.axis_size("blk") == 2
        if self.swap:
            self.take_rows(jnp.where(self.first(), other[:, :1], other[:, -1:]))
        else:
            self.send_rows()
            self.take_rows(*self.rows)

    def first(self):
        return lax.axis_index("blk") == 0

    def send_rows(self):
        head, tail = self.cells[:, :1], self.cells[:, -1:]
        if self.swap:
            rows = jnp.where(self.first(), tail, head)
            self.rows = [lax.ppermute(rows, "blk", [(0, 1), (1, 0)])]
        else:
            ends = lax.axis_size("blk") - 1
            self.rows = [
                lax.ppermute(tail, "blk", [(i, i + 1) for i in range(ends)]),
                lax.ppermute(head, "blk", [(i + 1, i) for i in range(ends)]),
            ]

    def take_rows(self, *rows):
        if self.swap:
            first = self.first()
            rows = [jnp.where(first, 0.0, rows[0]), jnp.where(first, rows[0], 0.0)]
        self.before, self.after = rows

    def make_layers(self, token):
        self.edges = edge_layers(self.cells, self.before, self.after, token)
        self.layers = []
        return self.edges[0]

    def send_layer(self, number):
        count = lax.axis_size("slab")
        pairs = []
        for low in range(number, count - 1, 2):
            pairs += [(low, low + 1), (low + 1, low)]
        self.layers.append(lax.ppermute(self.edges[number], "slab", pairs))

    def take_layers(self, token):
        layers = ordered(self.layers, token)
        odd = bit_of(lax.axis_index("slab"), 0) == 1
        below, above = jnp.where(odd, layers[0], layers[1]), jnp.where(odd, layers[1], layers[0])
        rows = self.cells.shape[1]
        cells = jnp.concatenate([below[:, :rows], self.cells, above[:, :rows]], axis=0)
        before = jnp.concatenate([below[:, rows : rows + 1], self.before, above[:, rows : rows + 1]], axis=0)
        after = jnp.concatenate([below[:, rows + 1 :], self.after, above[:, rows + 1 :]], axis=0)
        padded = jnp.concatenate([before, cells, after], axis=1)
        self.cells = sweep_once(pad_x(padded), self.sources, self.absorption)
        return layers[0]


def stiffness(padded):
    along_x = padded[:, :, :-2] + padded[:, :, 2:]
    middle = padded[:, :, 1:-1]
    plus_mid = along_x + middle
    plane_sum = plus_mid[:, :-2] + plus_mid[:, 1:-1] + plus_mid[:, 2:]
    total_sum = plane_sum[:-2] + plane_sum[1:-1] + plane_sum[2:]
    cross_xy = along_x[:, :-2] + along_x[:, 2:]
    corner_sum = cross_xy[:-2] + cross_xy[2:]
    face_sum = (
        along_x[1:-1, 1:-1]
        + middle[1:-1, :-2]
        + middle[1:-1, 2:]
        + middle[:-2, 1:-1]
        + middle[2:, 1:-1]
    )
    center = middle[1:-1, 1:-1]
    edge_sum = total_sum - center - face_sum - corner_sum
    return center_weight * center - edge_sum / 6.0 - corner_sum / 12.0


def sweep_once(padded, sources, absorption):
    center = padded[1:-1, 1:-1, 1:-1]
    applied = stiffness(padded) + absorption * center
    return center + omega * (sources - applied) / (center_weight + absorption)


def pad_x(values):
    return jnp.pad(values, ((0, 0), (0, 0), (1, 1)))


def per_device(interior, sources, absorption, bem_panel, incident, node_cell, offset):
    slab_count = lax.axis_size("slab")
    blk_count = lax.axis_size("blk")
    slab_cols, width = incident.shape
    panel_rows = bem_panel.shape[0]
    node_total = slab_cols * slab_count
    chunk_rows = panel_rows // slab_count
    bits = slab_count.bit_length() - 1

    if blk_count == 2:
        other = lax.ppermute(interior, "blk", [(0, 1), (1, 0)])
        interiors = [interior, other]
    else:
        other = None
        gathered = lax.all_gather(interior, "blk", axis=0)
        interiors = [gathered[i] for i in range(blk_count)]

    units, first, done = chunk_rows // ROW_UNIT, 0, 0
    spans = []
    for share, order in PIECES:
        done += share
        last = (units * done // 16) * ROW_UNIT
        if last > first:
            if bits != len(order):
                order = [(bit + len(spans)) % bits for bit in range(bits)]
            spans.append((first, last - first, order))
        first = last
    carrier = min(CARRIER, len(spans) - 1)
    pieces = [
        Piece(at, rows, order, TILE if number == carrier else 0)
        for number, (at, rows, order) in enumerate(spans)
    ]
    cells = node_cell.reshape(slab_cols // LANES, LANES)

    panel = bem_panel.reshape((2,) * bits + (chunk_rows, slab_cols))
    inside = Interior(interior, other, sources, absorption)
    inside.make_layers(offset)
    inside.send_layer(0)
    inside.send_layer(1)
    fields, squares, *far = first_products(
        [(piece, 0) for piece in pieces[:EARLY]], offset, interiors, cells, incident, panel
    )
    courses = [Course(piece, number, sent) for number, (piece, sent) in enumerate(zip(pieces, far))]
    token = far[0]
    events = EVENTS
    if len(pieces) * bits != sum(event.isdigit() for event in EVENTS):
        events = "F" * (len(pieces) - EARLY) + "Nabdc" + "".join(str(number) for number in range(len(pieces))) * bits
    for event in events:
        if event == "F":
            number = len(courses)
            token = later_products([(pieces[number], 0)], offset, fields, squares, panel, token)[0]
            courses.append(Course(pieces[number], number, token))
        elif event == "N":
            near = later_products([(piece, 1) for piece in pieces], offset, fields, squares, panel, token)
            token = near[0]
        elif event == "a":
            token = inside.take_layers(token)
            inside.send_rows()
        elif event == "b":
            inside.take_rows(*ordered(inside.rows, token))
            token = inside.make_layers(token)
            inside.send_layer(0)
        elif event == "d":
            inside.layers = list(ordered(inside.layers, token))
            inside.edges = ordered(inside.edges, inside.layers[0])
            inside.send_layer(1)
            token = inside.edges[0]
        elif event == "c":
            token = inside.take_layers(token)
        elif event.isdigit() and courses[int(event)].done is None:
            token = courses[int(event)].arrive(near[int(event)], token)
    owned = pl.pallas_call(
        functools.partial(finish_kernel, node_total, carrier, [piece.rows for piece in pieces]),
        in_specs=[IN_VMEM] * len(pieces),
        out_specs=IN_VMEM,
        out_shape=jax.ShapeDtypeStruct((chunk_rows, width), jnp.float32),
        compiler_params=PARAMS,
        cost_estimate=COST,
        name="divide_by_norms",
    )(*[course.done for course in courses])

    return (inside.cells, owned)


def solution(mesh):
    in_specs = (
        P("slab", "blk", None),
        P("slab", "blk", None),
        P("slab", "blk", None),
        P("blk", "slab"),
        P("slab", None),
        P("slab"),
        P(),
    )
    out_specs = (P("slab", "blk", None), P(("blk", "slab"), None))
    return jax.shard_map(
        per_device, mesh=mesh, in_specs=in_specs, out_specs=out_specs, check_vma=False
    )
```

```python
import functools

import jax
import jax.numpy as jnp
from jax import lax
from jax.experimental import pallas as pl
from jax.experimental.pallas import tpu as pltpu
from jax.sharding import PartitionSpec as P

SWEEPS = 2

omega = 0.6
center_weight = 8.0 / 3.0
LANES = 128
ROW_UNIT = 16
TILE = 8
LIMIT = 16 * 2**20

PIECES = ((4, (0, 1, 3, 2)), (4, (1, 0, 2, 3)), (6, (2, 1, 0, 3)), (2, (0, 2, 1, 3)))
EARLY = 3
CARRIER = 0
EVENTS = "abFN0d123031203103c212"


def bit_of(slab, bit):
    return (slab >> bit) & 1


class Piece:
    def __init__(self, first, rows, order, extra):
        self.first, self.rows, self.order, self.extra = first, rows, order, extra
        self.bits = len(order)

    def height(self, blocks):
        return blocks * self.rows + self.extra

    def halves(self, step, slab):
        left = [bit for bit in range(self.bits) if bit not in self.order[:step]]
        inner = 1 << left.index(self.order[step])
        outer = (1 << len(left)) // (2 * inner)
        own = bit_of(slab, self.order[step])
        return [
            [i * (2 * inner) + half * inner + j for i in range(outer) for j in range(inner)]
            for half in (1 - own, own)
        ]

    def window(self, which, slab):
        index = [slice(None)] * self.bits
        own = bit_of(slab, self.order[0])
        index[self.bits - 1 - self.order[0]] = own if which else 1 - own
        return tuple(index) + (pl.ds(self.first, self.rows), slice(None))

    def window_shape(self):
        return (2,) * (self.bits - 1) + (self.rows,)

    def pairs(self, step):
        return [(i, i ^ (1 << self.order[step])) for i in range(1 << self.bits)]


def panel_copies(jobs, panel, panel_bufs, sems):
    slab = lax.axis_index("slab")
    started = []
    for number, (piece, which) in enumerate(jobs):
        copy = pltpu.make_async_copy(
            panel.at[piece.window(which, slab)], panel_bufs[number], sems.at[number]
        )
        copy.start()
        started.append((piece, piece.halves(0, slab)[which], copy, panel_bufs[number]))
    return started


def multiply(jobs, shift, chunk_rows, fields, squares, outs):
    node_count, width = fields.shape
    for (piece, chunks, copy, panel_buf), out in zip(jobs, outs):
        copy.wait()
        rows = piece.rows
        lhs = panel_buf[...].reshape(len(chunks) * rows, node_count)
        product = jnp.dot(lhs, fields[...], preferred_element_type=jnp.float32)
        for block, chunk in enumerate(chunks):
            at = block * rows
            out[at : at + rows, :] = product[at : at + rows]
            node = shift + chunk * chunk_rows

            @pl.when((node >= 0) & (node < node_count))
            def _(at=at, node=node):
                first = pl.multiple_of(node + piece.first, ROW_UNIT)
                jump = fields[pl.ds(first, rows), :].astype(jnp.float32)
                out[at : at + rows, :] += 0.5 * jump

        if piece.extra:
            row = lax.broadcasted_iota(jnp.int32, (TILE, width), 0)
            at = len(chunks) * rows
            out[at : at + TILE, :] = jnp.where(row == 0, squares[...], 0.0)


def make_fields(blk, interiors, cells, incident, fields, squares):
    tables = []
    for block in interiors:
        depth_z, depth_y, width = block.shape
        flat_left = block[:, :, :LANES].reshape(depth_z * depth_y, LANES)
        flat_right = block[:, :, width - LANES :].reshape(depth_z * depth_y, LANES)
        tables.append((flat_left.T[0:1, :], flat_right.T[LANES - 1 : LANES, :]))
    node_count = incident.shape[0]
    per_block = node_count // (2 if len(interiors) == 2 else len(interiors))
    across = cells[...].T
    lane = lax.broadcasted_iota(jnp.int32, (LANES, tables[0][0].shape[1]), 1)
    total = jnp.zeros((8, incident.shape[1]), jnp.float32)
    for part in range(node_count // LANES):
        owner = part * LANES // per_block
        if len(interiors) == 2:
            mine = blk == owner
            left = jnp.where(mine, tables[0][0], tables[1][0])
            right = jnp.where(mine, tables[0][1], tables[1][1])
        else:
            left, right = tables[owner]
        cell = across[:, part : part + 1]
        column = cell >> 1
        value = jnp.where((cell & 1) == 1, right, left)
        trace = jnp.sum(jnp.where(lane == column, value, 0.0), axis=1, keepdims=True)
        rows = pl.ds(part * LANES, LANES)
        field = (incident[rows, :].astype(jnp.float32) + trace).astype(jnp.bfloat16)
        fields[rows, :] = field
        wide = field.astype(jnp.float32)
        total = total + jnp.sum((wide * wide).reshape(LANES // 8, 8, wide.shape[1]), axis=0)
    squares[...] = jnp.sum(total, axis=0, keepdims=True)


def shift_of(offset, panel_rows, node_count):
    return (
        offset[0] + lax.axis_index("blk") * panel_rows - lax.axis_index("slab") * node_count
    )


def first_kernel(jobs, blocks, offset, *refs):
    interiors, refs = refs[:blocks], refs[blocks:]
    cells, incident, panel, fields, squares = refs[:5]
    count = len(jobs)
    outs, refs = refs[5 : 5 + count], refs[5 + count :]
    panel_bufs, refs = refs[:count], refs[count:]
    interior_bufs, refs = refs[:blocks], refs[blocks:]
    cells_buf, incident_buf, sems, in_sems = refs
    copies = []
    for number, (source, target) in enumerate(zip(list(interiors) + [cells, incident], list(interior_bufs) + [cells_buf, incident_buf])):
        copy = pltpu.make_async_copy(source, target, in_sems.at[number])
        copy.start()
        copies.append(copy)
    started = panel_copies(jobs, panel, panel_bufs, sems)
    for copy in copies:
        copy.wait()
    make_fields(lax.axis_index("blk"), interior_bufs, cells_buf, incident_buf, fields, squares)
    chunk_rows = panel.shape[-2]
    shift = shift_of(offset, chunk_rows * lax.axis_size("slab"), incident.shape[0])
    multiply(started, shift, chunk_rows, fields, squares, outs)


def later_kernel(jobs, offset, fields, squares, panel, token, *refs):
    count = len(jobs)
    outs, panel_bufs = refs[:count], refs[count : 2 * count]
    sems = refs[2 * count]
    started = panel_copies(jobs, panel, panel_bufs, sems)
    chunk_rows = panel.shape[-2]
    shift = shift_of(offset, chunk_rows * lax.axis_size("slab"), fields.shape[0])
    multiply(started, shift, chunk_rows, fields, squares, outs)


def piece_scratch(jobs, depth):
    return [
        pltpu.VMEM(piece.window_shape() + (depth,), jnp.bfloat16) for piece, _ in jobs
    ], pltpu.SemaphoreType.DMA((len(jobs),))


def piece_shapes(jobs, width):
    return [
        pltpu.VMEM((piece.height(len(piece.halves(0, 0)[0])), width), jnp.float32) for piece, _ in jobs
    ]


COST = pl.CostEstimate(flops=1, bytes_accessed=1, transcendentals=0)

IN_HBM = pl.BlockSpec(memory_space=pltpu.HBM)
ANYWHERE = pl.BlockSpec(memory_space=pl.ANY)
IN_VMEM = pl.BlockSpec(memory_space=pltpu.VMEM)
IN_SMEM = pl.BlockSpec(memory_space=pltpu.SMEM)
PARAMS = pltpu.CompilerParams(vmem_limit_bytes=LIMIT)


def in_hbm(array):
    return pltpu.with_memory_space_constraint(array, pltpu.HBM)


def first_products(jobs, offset, interiors, cells, incident, panel):
    depth, width = incident.shape
    bufs, sems = piece_scratch(jobs, depth)
    return pl.pallas_call(
        functools.partial(first_kernel, jobs, len(interiors)),
        in_specs=[IN_SMEM] + [ANYWHERE] * len(interiors) + [IN_HBM] * 3,
        out_specs=[IN_VMEM] * (2 + len(jobs)),
        out_shape=[pltpu.VMEM(incident.shape, jnp.bfloat16), pltpu.VMEM((1, width), jnp.float32)]
        + piece_shapes(jobs, width),
        scratch_shapes=bufs
        + [pltpu.VMEM(array.shape, array.dtype) for array in (*interiors, cells, incident)]
        + [sems, pltpu.SemaphoreType.DMA((len(interiors) + 2,))],
        compiler_params=PARAMS,
        cost_estimate=COST,
        name="fields_and_first_rows",
    )(offset, in_hbm(interiors[0]), *interiors[1:], in_hbm(cells), in_hbm(incident), in_hbm(panel))


def later_products(jobs, offset, fields, squares, panel, token):
    depth, width = fields.shape
    bufs, sems = piece_scratch(jobs, depth)
    return pl.pallas_call(
        functools.partial(later_kernel, jobs),
        in_specs=[IN_SMEM, IN_VMEM, IN_VMEM, IN_HBM, ANYWHERE],
        out_specs=[IN_VMEM] * len(jobs),
        out_shape=piece_shapes(jobs, width),
        scratch_shapes=bufs + [sems],
        compiler_params=PARAMS,
        cost_estimate=COST,
        name="other_rows",
    )(offset, fields, squares, in_hbm(panel), token)


def arrival_kernel(piece, step, got, base, token, *outs):
    rows, extra = piece.rows, piece.extra
    halves = [[0]] if step == piece.bits else piece.halves(step, lax.axis_index("slab"))
    for blocks, out in zip(halves, outs):
        for number, block in enumerate(blocks):
            here = pl.ds(pl.multiple_of(block * rows, TILE), rows)
            out[number * rows : (number + 1) * rows, :] = got[here, :] + base[here, :]
        if extra:
            last = base.shape[0] - extra
            at = len(blocks) * rows
            out[at : at + extra, :] = got[last:, :] + base[last:, :]


def add_arrival(piece, step, got, base, token, name):
    count = 1 if step == piece.bits else 2
    blocks = max(1, (1 << piece.bits) >> (step + 1))
    shape = pltpu.VMEM((piece.height(blocks), base.shape[1]), jnp.float32)
    return pl.pallas_call(
        functools.partial(arrival_kernel, piece, step),
        in_specs=[IN_VMEM, IN_VMEM, ANYWHERE],
        out_specs=[IN_VMEM] * count,
        out_shape=[shape] * count,
        compiler_params=PARAMS,
        cost_estimate=COST,
        name=name,
    )(got, base, token)


class Course:
    def __init__(self, piece, number, far):
        self.piece, self.number = piece, number
        self.step, self.near, self.done = 0, None, None
        self.send(far)

    def send(self, rows):
        self.got = lax.ppermute(rows, "slab", self.piece.pairs(self.step))

    def arrive(self, kept, token):
        base = kept if self.step == 0 else self.near
        self.step += 1
        name = f"arrival_{self.number}_{self.step}"
        outs = add_arrival(self.piece, self.step, self.got, base, token, name)
        if self.step == self.piece.bits:
            self.done = outs[0]
        else:
            self.near = outs[1]
            self.send(outs[0])
        return outs[0]


def finish_kernel(node_total, carrier, rows, *refs):
    parts, out = refs[:-1], refs[-1]
    squares = parts[carrier][rows[carrier] : rows[carrier] + 1, :]
    norms = jnp.sqrt(squares / node_total + 1e-06)
    first = 0
    for part, height in zip(parts, rows):
        out[first : first + height, :] = part[:height, :] / norms
        first += height


def ordered_kernel(count, *refs):
    for source, target in zip(refs[:count], refs[count + 1 :]):
        target[...] = source[...]


def ordered(arrays, token):
    return pl.pallas_call(
        functools.partial(ordered_kernel, len(arrays)),
        in_specs=[IN_VMEM] * len(arrays) + [ANYWHERE],
        out_specs=[IN_VMEM] * len(arrays),
        out_shape=[pltpu.VMEM(array.shape, array.dtype) for array in arrays],
        compiler_params=PARAMS,
        cost_estimate=COST,
        name="ordered",
    )(*arrays, token)


def edge_kernel(cells, before, after, *outs):
    depth, rows = cells.shape[:2]
    odd = bit_of(lax.axis_index("slab"), 0)
    for layer, lowest in zip(outs, (odd, 1 - odd)):
        at = (1 - lowest) * (depth - 1)
        layer[0, 0:rows, :] = cells[at]
        layer[0, rows : rows + 1, :] = before[at]
        layer[0, rows + 1 : rows + 2, :] = after[at]


def edge_copies_kernel(cells, before, after, token, *refs):
    outs, bufs, sems = refs[:2], refs[2], refs[3]
    depth, rows = cells.shape[:2]
    odd = bit_of(lax.axis_index("slab"), 0)
    copies = []
    for number, lowest in enumerate((odd, 1 - odd)):
        at = (1 - lowest) * (depth - 1)
        copy = pltpu.make_async_copy(cells.at[at], bufs.at[number], sems.at[number])
        copy.start()
        copies.append((copy, at))
    for number, (layer, (copy, at)) in enumerate(zip(outs, copies)):
        copy.wait()
        layer[0, 0:rows, :] = bufs[number]
        layer[0, rows : rows + 1, :] = before[at]
        layer[0, rows + 1 : rows + 2, :] = after[at]


def first_layers(cells, before, after, token):
    shape = pltpu.VMEM((1, cells.shape[1] + 2, cells.shape[2]), jnp.float32)
    return pl.pallas_call(
        edge_copies_kernel,
        in_specs=[IN_HBM] + [IN_VMEM] * 2 + [ANYWHERE],
        out_specs=[IN_VMEM] * 2,
        out_shape=[shape, shape],
        scratch_shapes=[pltpu.VMEM((2,) + cells.shape[1:], jnp.float32), pltpu.SemaphoreType.DMA((2,))],
        compiler_params=PARAMS,
        cost_estimate=COST,
        name="first_layers",
    )(in_hbm(cells), before, after, token)


def edge_layers(cells, before, after, token):
    shape = pltpu.VMEM((1, cells.shape[1] + 2, cells.shape[2]), jnp.float32)
    return pl.pallas_call(
        lambda cells, before, after, token, *outs: edge_kernel(cells, before, after, *outs),
        in_specs=[IN_VMEM] * 3 + [ANYWHERE],
        out_specs=[IN_VMEM] * 2,
        out_shape=[shape, shape],
        compiler_params=PARAMS,
        cost_estimate=COST,
        name="edge_layers",
    )(cells, before, after, token)


class Interior:
    def __init__(self, interior, other, sources, absorption):
        self.cells, self.sources, self.absorption = interior, sources, absorption
        self.swap = lax.axis_size("blk") == 2
        if self.swap:
            self.take_rows(jnp.where(self.first(), other[:, :1], other[:, -1:]))
        else:
            self.send_rows()
            self.take_rows(*self.rows)

    def first(self):
        return lax.axis_index("blk") == 0

    def send_rows(self):
        head, tail = self.cells[:, :1], self.cells[:, -1:]
        if self.swap:
            rows = jnp.where(self.first(), tail, head)
            self.rows = [lax.ppermute(rows, "blk", [(0, 1), (1, 0)])]
        else:
            ends = lax.axis_size("blk") - 1
            self.rows = [
                lax.ppermute(tail, "blk", [(i, i + 1) for i in range(ends)]),
                lax.ppermute(head, "blk", [(i + 1, i) for i in range(ends)]),
            ]

    def take_rows(self, *rows):
        if self.swap:
            first = self.first()
            rows = [jnp.where(first, 0.0, rows[0]), jnp.where(first, rows[0], 0.0)]
        self.before, self.after = rows

    def make_layers(self, token, make=edge_layers):
        self.edges = make(self.cells, self.before, self.after, token)
        self.layers = []
        return self.edges[0]

    def send_layer(self, number):
        count = lax.axis_size("slab")
        pairs = []
        for low in range(number, count - 1, 2):
            pairs += [(low, low + 1), (low + 1, low)]
        self.layers.append(lax.ppermute(self.edges[number], "slab", pairs))

    def take_layers(self, token):
        layers = ordered(self.layers, token)
        odd = bit_of(lax.axis_index("slab"), 0) == 1
        below, above = jnp.where(odd, layers[0], layers[1]), jnp.where(odd, layers[1], layers[0])
        rows = self.cells.shape[1]
        cells = jnp.concatenate([below[:, :rows], self.cells, above[:, :rows]], axis=0)
        before = jnp.concatenate([below[:, rows : rows + 1], self.before, above[:, rows : rows + 1]], axis=0)
        after = jnp.concatenate([below[:, rows + 1 :], self.after, above[:, rows + 1 :]], axis=0)
        padded = jnp.concatenate([before, cells, after], axis=1)
        self.cells = sweep_once(pad_x(padded), self.sources, self.absorption)
        return layers[0]


def stiffness(padded):
    along_x = padded[:, :, :-2] + padded[:, :, 2:]
    middle = padded[:, :, 1:-1]
    plus_mid = along_x + middle
    plane_sum = plus_mid[:, :-2] + plus_mid[:, 1:-1] + plus_mid[:, 2:]
    total_sum = plane_sum[:-2] + plane_sum[1:-1] + plane_sum[2:]
    cross_xy = along_x[:, :-2] + along_x[:, 2:]
    corner_sum = cross_xy[:-2] + cross_xy[2:]
    face_sum = (
        along_x[1:-1, 1:-1]
        + middle[1:-1, :-2]
        + middle[1:-1, 2:]
        + middle[:-2, 1:-1]
        + middle[2:, 1:-1]
    )
    center = middle[1:-1, 1:-1]
    edge_sum = total_sum - center - face_sum - corner_sum
    return center_weight * center - edge_sum / 6.0 - corner_sum / 12.0


def sweep_once(padded, sources, absorption):
    center = padded[1:-1, 1:-1, 1:-1]
    applied = stiffness(padded) + absorption * center
    return center + omega * (sources - applied) / (center_weight + absorption)


def pad_x(values):
    return jnp.pad(values, ((0, 0), (0, 0), (1, 1)))


def per_device(interior, sources, absorption, bem_panel, incident, node_cell, offset):
    slab_count = lax.axis_size("slab")
    blk_count = lax.axis_size("blk")
    slab_cols, width = incident.shape
    panel_rows = bem_panel.shape[0]
    node_total = slab_cols * slab_count
    chunk_rows = panel_rows // slab_count
    bits = slab_count.bit_length() - 1

    if blk_count == 2:
        other = lax.ppermute(interior, "blk", [(0, 1), (1, 0)])
        interiors = [interior, other]
    else:
        other = None
        gathered = lax.all_gather(interior, "blk", axis=0)
        interiors = [gathered[i] for i in range(blk_count)]

    units, first, done = chunk_rows // ROW_UNIT, 0, 0
    spans = []
    for share, order in PIECES:
        done += share
        last = (units * done // 16) * ROW_UNIT
        if last > first:
            if bits != len(order):
                order = [(bit + len(spans)) % bits for bit in range(bits)]
            spans.append((first, last - first, order))
        first = last
    carrier = min(CARRIER, len(spans) - 1)
    pieces = [
        Piece(at, rows, order, TILE if number == carrier else 0)
        for number, (at, rows, order) in enumerate(spans)
    ]
    cells = node_cell.reshape(slab_cols // LANES, LANES)

    panel = bem_panel.reshape((2,) * bits + (chunk_rows, slab_cols))
    inside = Interior(interior, other, sources, absorption)
    inside.make_layers(offset, first_layers)
    inside.send_layer(0)
    inside.send_layer(1)
    fields, squares, *far = first_products(
        [(piece, 0) for piece in pieces[:EARLY]], offset, interiors, cells, incident, panel
    )
    courses = [Course(piece, number, sent) for number, (piece, sent) in enumerate(zip(pieces, far))]
    token = far[0]
    events = EVENTS
    if len(pieces) * bits != sum(event.isdigit() for event in EVENTS):
        events = "F" * (len(pieces) - EARLY) + "Nabdc" + "".join(str(number) for number in range(len(pieces))) * bits
    for event in events:
        if event == "F":
            number = len(courses)
            token = later_products([(pieces[number], 0)], offset, fields, squares, panel, token)[0]
            courses.append(Course(pieces[number], number, token))
        elif event == "N":
            near = later_products([(piece, 1) for piece in pieces], offset, fields, squares, panel, token)
            token = near[0]
        elif event == "a":
            token = inside.take_layers(token)
            inside.send_rows()
        elif event == "b":
            inside.take_rows(*ordered(inside.rows, token))
            token = inside.make_layers(token)
            inside.send_layer(0)
        elif event == "d":
            inside.layers = list(ordered(inside.layers, token))
            inside.edges = ordered(inside.edges, inside.layers[0])
            inside.send_layer(1)
            token = inside.edges[0]
        elif event == "c":
            token = inside.take_layers(token)
        elif event.isdigit() and courses[int(event)].done is None:
            token = courses[int(event)].arrive(near[int(event)], token)
    owned = pl.pallas_call(
        functools.partial(finish_kernel, node_total, carrier, [piece.rows for piece in pieces]),
        in_specs=[IN_VMEM] * len(pieces),
        out_specs=IN_VMEM,
        out_shape=jax.ShapeDtypeStruct((chunk_rows, width), jnp.float32),
        compiler_params=PARAMS,
        cost_estimate=COST,
        name="divide_by_norms",
    )(*[course.done for course in courses])

    return (inside.cells, owned)


def solution(mesh):
    in_specs = (
        P("slab", "blk", None),
        P("slab", "blk", None),
        P("slab", "blk", None),
        P("blk", "slab"),
        P("slab", None),
        P("slab"),
        P(),
    )
    out_specs = (P("slab", "blk", None), P(("blk", "slab"), None))
    return jax.shard_map(
        per_device, mesh=mesh, in_specs=in_specs, out_specs=out_specs, check_vma=False
    )
```

```python
import functools

import jax
import jax.numpy as jnp
from jax import lax
from jax.experimental import pallas as pl
from jax.experimental.pallas import tpu as pltpu
from jax.sharding import PartitionSpec as P

SWEEPS = 2

omega = 0.6
center_weight = 8.0 / 3.0
LANES = 128
ROW_UNIT = 16
TILE = 8
LIMIT = 16 * 2**20

PIECES = ((4, (0, 1, 3, 2)), (4, (1, 0, 2, 3)), (6, (2, 1, 0, 3)), (2, (0, 2, 1, 3)))
EARLY = 3
CARRIER = 0
EVENTS = "abFN0d123031203103c212"


def bit_of(slab, bit):
    return (slab >> bit) & 1


class Piece:
    def __init__(self, first, rows, order, extra):
        self.first, self.rows, self.order, self.extra = first, rows, order, extra
        self.bits = len(order)

    def height(self, blocks):
        return blocks * self.rows + self.extra

    def halves(self, step, slab):
        left = [bit for bit in range(self.bits) if bit not in self.order[:step]]
        inner = 1 << left.index(self.order[step])
        outer = (1 << len(left)) // (2 * inner)
        own = bit_of(slab, self.order[step])
        return [
            [i * (2 * inner) + half * inner + j for i in range(outer) for j in range(inner)]
            for half in (1 - own, own)
        ]

    def window(self, which, slab):
        index = [slice(None)] * self.bits
        own = bit_of(slab, self.order[0])
        index[self.bits - 1 - self.order[0]] = own if which else 1 - own
        return tuple(index) + (pl.ds(self.first, self.rows), slice(None))

    def window_shape(self):
        return (2,) * (self.bits - 1) + (self.rows,)

    def pairs(self, step):
        return [(i, i ^ (1 << self.order[step])) for i in range(1 << self.bits)]


def panel_copies(jobs, panel, panel_bufs, sems):
    slab = lax.axis_index("slab")
    started = []
    for number, (piece, which) in enumerate(jobs):
        copy = pltpu.make_async_copy(
            panel.at[piece.window(which, slab)], panel_bufs[number], sems.at[number]
        )
        copy.start()
        started.append((piece, piece.halves(0, slab)[which], copy, panel_bufs[number]))
    return started


def multiply(jobs, shift, chunk_rows, fields, squares, outs):
    node_count, width = fields.shape
    for (piece, chunks, copy, panel_buf), out in zip(jobs, outs):
        copy.wait()
        rows = piece.rows
        lhs = panel_buf[...].reshape(len(chunks) * rows, node_count)
        product = jnp.dot(lhs, fields[...], preferred_element_type=jnp.float32)
        for block, chunk in enumerate(chunks):
            at = block * rows
            out[at : at + rows, :] = product[at : at + rows]
            node = shift + chunk * chunk_rows

            @pl.when((node >= 0) & (node < node_count))
            def _(at=at, node=node):
                first = pl.multiple_of(node + piece.first, ROW_UNIT)
                jump = fields[pl.ds(first, rows), :].astype(jnp.float32)
                out[at : at + rows, :] += 0.5 * jump

        if piece.extra:
            row = lax.broadcasted_iota(jnp.int32, (TILE, width), 0)
            at = len(chunks) * rows
            out[at : at + TILE, :] = jnp.where(row == 0, squares[...], 0.0)


def make_fields(blk, interiors, cells, incident, fields, squares):
    tables = []
    for block in interiors:
        depth_z, depth_y, width = block.shape
        flat_left = block[:, :, :LANES].reshape(depth_z * depth_y, LANES)
        flat_right = block[:, :, width - LANES :].reshape(depth_z * depth_y, LANES)
        tables.append((flat_left.T[0:1, :], flat_right.T[LANES - 1 : LANES, :]))
    node_count = incident.shape[0]
    per_block = node_count // (2 if len(interiors) == 2 else len(interiors))
    across = cells[...].T
    lane = lax.broadcasted_iota(jnp.int32, (LANES, tables[0][0].shape[1]), 1)
    total = jnp.zeros((8, incident.shape[1]), jnp.float32)
    for part in range(node_count // LANES):
        owner = part * LANES // per_block
        if len(interiors) == 2:
            mine = blk == owner
            left = jnp.where(mine, tables[0][0], tables[1][0])
            right = jnp.where(mine, tables[0][1], tables[1][1])
        else:
            left, right = tables[owner]
        cell = across[:, part : part + 1]
        column = cell >> 1
        value = jnp.where((cell & 1) == 1, right, left)
        trace = jnp.sum(jnp.where(lane == column, value, 0.0), axis=1, keepdims=True)
        rows = pl.ds(part * LANES, LANES)
        field = (incident[rows, :].astype(jnp.float32) + trace).astype(jnp.bfloat16)
        fields[rows, :] = field
        wide = field.astype(jnp.float32)
        total = total + jnp.sum((wide * wide).reshape(LANES // 8, 8, wide.shape[1]), axis=0)
    squares[...] = jnp.sum(total, axis=0, keepdims=True)


def shift_of(offset, panel_rows, node_count):
    return (
        offset[0] + lax.axis_index("blk") * panel_rows - lax.axis_index("slab") * node_count
    )


def first_kernel(jobs, blocks, offset, *refs):
    interiors, refs = refs[:blocks], refs[blocks:]
    cells, incident, panel, fields, squares = refs[:5]
    count = len(jobs)
    outs, refs = refs[5 : 5 + count], refs[5 + count :]
    panel_bufs, refs = refs[:count], refs[count:]
    interior_bufs, refs = refs[:blocks], refs[blocks:]
    cells_buf, incident_buf, sems, in_sems = refs
    copies = []
    for number, (source, target) in enumerate(zip(list(interiors) + [cells, incident], list(interior_bufs) + [cells_buf, incident_buf])):
        copy = pltpu.make_async_copy(source, target, in_sems.at[number])
        copy.start()
        copies.append(copy)
    started = panel_copies(jobs, panel, panel_bufs, sems)
    for copy in copies:
        copy.wait()
    make_fields(lax.axis_index("blk"), interior_bufs, cells_buf, incident_buf, fields, squares)
    chunk_rows = panel.shape[-2]
    shift = shift_of(offset, chunk_rows * lax.axis_size("slab"), incident.shape[0])
    multiply(started, shift, chunk_rows, fields, squares, outs)


def later_kernel(jobs, offset, fields, squares, panel, token, *refs):
    count = len(jobs)
    outs, panel_bufs = refs[:count], refs[count : 2 * count]
    sems = refs[2 * count]
    started = panel_copies(jobs, panel, panel_bufs, sems)
    chunk_rows = panel.shape[-2]
    shift = shift_of(offset, chunk_rows * lax.axis_size("slab"), fields.shape[0])
    multiply(started, shift, chunk_rows, fields, squares, outs)


def piece_scratch(jobs, depth):
    return [
        pltpu.VMEM(piece.window_shape() + (depth,), jnp.bfloat16) for piece, _ in jobs
    ], pltpu.SemaphoreType.DMA((len(jobs),))


def piece_shapes(jobs, width):
    return [
        pltpu.VMEM((piece.height(len(piece.halves(0, 0)[0])), width), jnp.float32) for piece, _ in jobs
    ]


COST = pl.CostEstimate(flops=1, bytes_accessed=1, transcendentals=0)

IN_HBM = pl.BlockSpec(memory_space=pltpu.HBM)
ANYWHERE = pl.BlockSpec(memory_space=pl.ANY)
IN_VMEM = pl.BlockSpec(memory_space=pltpu.VMEM)
IN_SMEM = pl.BlockSpec(memory_space=pltpu.SMEM)
PARAMS = pltpu.CompilerParams(vmem_limit_bytes=LIMIT)


def in_hbm(array):
    return pltpu.with_memory_space_constraint(array, pltpu.HBM)


def first_products(jobs, offset, interiors, cells, incident, panel):
    depth, width = incident.shape
    bufs, sems = piece_scratch(jobs, depth)
    return pl.pallas_call(
        functools.partial(first_kernel, jobs, len(interiors)),
        in_specs=[IN_SMEM] + [ANYWHERE] * len(interiors) + [IN_HBM] * 3,
        out_specs=[IN_VMEM] * (2 + len(jobs)),
        out_shape=[pltpu.VMEM(incident.shape, jnp.bfloat16), pltpu.VMEM((1, width), jnp.float32)]
        + piece_shapes(jobs, width),
        scratch_shapes=bufs
        + [pltpu.VMEM(array.shape, array.dtype) for array in (*interiors, cells, incident)]
        + [sems, pltpu.SemaphoreType.DMA((len(interiors) + 2,))],
        compiler_params=PARAMS,
        cost_estimate=COST,
        name="fields_and_first_rows",
    )(offset, in_hbm(interiors[0]), *interiors[1:], in_hbm(cells), in_hbm(incident), in_hbm(panel))


def later_products(jobs, offset, fields, squares, panel, token):
    depth, width = fields.shape
    bufs, sems = piece_scratch(jobs, depth)
    return pl.pallas_call(
        functools.partial(later_kernel, jobs),
        in_specs=[IN_SMEM, IN_VMEM, IN_VMEM, IN_HBM, ANYWHERE],
        out_specs=[IN_VMEM] * len(jobs),
        out_shape=piece_shapes(jobs, width),
        scratch_shapes=bufs + [sems],
        compiler_params=PARAMS,
        cost_estimate=COST,
        name="other_rows",
    )(offset, fields, squares, in_hbm(panel), token)


def arrival_kernel(piece, step, got, base, token, *outs):
    rows, extra = piece.rows, piece.extra
    halves = [[0]] if step == piece.bits else piece.halves(step, lax.axis_index("slab"))
    for blocks, out in zip(halves, outs):
        for number, block in enumerate(blocks):
            here = pl.ds(pl.multiple_of(block * rows, TILE), rows)
            out[number * rows : (number + 1) * rows, :] = got[here, :] + base[here, :]
        if extra:
            last = base.shape[0] - extra
            at = len(blocks) * rows
            out[at : at + extra, :] = got[last:, :] + base[last:, :]


def add_arrival(piece, step, got, base, token, name):
    count = 1 if step == piece.bits else 2
    blocks = max(1, (1 << piece.bits) >> (step + 1))
    shape = pltpu.VMEM((piece.height(blocks), base.shape[1]), jnp.float32)
    return pl.pallas_call(
        functools.partial(arrival_kernel, piece, step),
        in_specs=[IN_VMEM, IN_VMEM, ANYWHERE],
        out_specs=[IN_VMEM] * count,
        out_shape=[shape] * count,
        compiler_params=PARAMS,
        cost_estimate=COST,
        name=name,
    )(got, base, token)


class Course:
    def __init__(self, piece, number, far):
        self.piece, self.number = piece, number
        self.step, self.near, self.done = 0, None, None
        self.send(far)

    def send(self, rows):
        self.got = lax.ppermute(rows, "slab", self.piece.pairs(self.step))

    def arrive(self, kept, token):
        base = kept if self.step == 0 else self.near
        self.step += 1
        name = f"arrival_{self.number}_{self.step}"
        outs = add_arrival(self.piece, self.step, self.got, base, token, name)
        if self.step == self.piece.bits:
            self.done = outs[0]
        else:
            self.near = outs[1]
            self.send(outs[0])
        return outs[0]


def finish_kernel(node_total, carrier, rows, *refs):
    parts, out = refs[:-1], refs[-1]
    squares = parts[carrier][rows[carrier] : rows[carrier] + 1, :]
    norms = jnp.sqrt(squares / node_total + 1e-06)
    first = 0
    for part, height in zip(parts, rows):
        out[first : first + height, :] = part[:height, :] / norms
        first += height


def ordered_kernel(count, *refs):
    for source, target in zip(refs[:count], refs[count + 1 :]):
        target[...] = source[...]


def ordered(arrays, token):
    return pl.pallas_call(
        functools.partial(ordered_kernel, len(arrays)),
        in_specs=[IN_VMEM] * len(arrays) + [ANYWHERE],
        out_specs=[IN_VMEM] * len(arrays),
        out_shape=[pltpu.VMEM(array.shape, array.dtype) for array in arrays],
        compiler_params=PARAMS,
        cost_estimate=COST,
        name="ordered",
    )(*arrays, token)


def edge_kernel(cells, before, after, *outs):
    depth, rows = cells.shape[:2]
    odd = bit_of(lax.axis_index("slab"), 0)
    for layer, lowest in zip(outs, (odd, 1 - odd)):
        at = (1 - lowest) * (depth - 1)
        layer[0, 0:rows, :] = cells[at]
        layer[0, rows : rows + 1, :] = before[at]
        layer[0, rows + 1 : rows + 2, :] = after[at]


def edge_copies_kernel(cells, before, after, token, *refs):
    outs, bufs, sems = refs[:2], refs[2], refs[3]
    depth, rows = cells.shape[:2]
    odd = bit_of(lax.axis_index("slab"), 0)
    copies = []
    for number, lowest in enumerate((odd, 1 - odd)):
        at = (1 - lowest) * (depth - 1)
        copy = pltpu.make_async_copy(cells.at[at], bufs.at[number], sems.at[number])
        copy.start()
        copies.append((copy, at))
    for number, (layer, (copy, at)) in enumerate(zip(outs, copies)):
        copy.wait()
        layer[0, 0:rows, :] = bufs[number]
        layer[0, rows : rows + 1, :] = before[at]
        layer[0, rows + 1 : rows + 2, :] = after[at]


def first_layers(cells, before, after, token):
    shape = pltpu.VMEM((1, cells.shape[1] + 2, cells.shape[2]), jnp.float32)
    return pl.pallas_call(
        edge_copies_kernel,
        in_specs=[IN_HBM] + [IN_VMEM] * 2 + [ANYWHERE],
        out_specs=[IN_VMEM] * 2,
        out_shape=[shape, shape],
        scratch_shapes=[pltpu.VMEM((2,) + cells.shape[1:], jnp.float32), pltpu.SemaphoreType.DMA((2,))],
        compiler_params=PARAMS,
        cost_estimate=COST,
        name="first_layers",
    )(in_hbm(cells), before, after, token)


def edge_layers(cells, before, after, token):
    shape = pltpu.VMEM((1, cells.shape[1] + 2, cells.shape[2]), jnp.float32)
    return pl.pallas_call(
        lambda cells, before, after, token, *outs: edge_kernel(cells, before, after, *outs),
        in_specs=[IN_VMEM] * 3 + [ANYWHERE],
        out_specs=[IN_VMEM] * 2,
        out_shape=[shape, shape],
        compiler_params=PARAMS,
        cost_estimate=COST,
        name="edge_layers",
    )(cells, before, after, token)


class Interior:
    def __init__(self, interior, other, sources, absorption):
        self.cells, self.sources, self.absorption = interior, sources, absorption
        self.swap = lax.axis_size("blk") == 2
        if self.swap:
            self.take_rows(jnp.where(self.first(), other[:, :1], other[:, -1:]))
        else:
            self.send_rows()
            self.take_rows(*self.rows)

    def first(self):
        return lax.axis_index("blk") == 0

    def send_rows(self):
        head, tail = self.cells[:, :1], self.cells[:, -1:]
        if self.swap:
            rows = jnp.where(self.first(), tail, head)
            self.rows = [lax.ppermute(rows, "blk", [(0, 1), (1, 0)])]
        else:
            ends = lax.axis_size("blk") - 1
            self.rows = [
                lax.ppermute(tail, "blk", [(i, i + 1) for i in range(ends)]),
                lax.ppermute(head, "blk", [(i + 1, i) for i in range(ends)]),
            ]

    def take_rows(self, *rows):
        if self.swap:
            first = self.first()
            rows = [jnp.where(first, 0.0, rows[0]), jnp.where(first, rows[0], 0.0)]
        self.before, self.after = rows

    def make_layers(self, token, make=edge_layers):
        self.edges = make(self.cells, self.before, self.after, token)
        self.layers = []
        return self.edges[0]

    def send_layer(self, number):
        count = lax.axis_size("slab")
        pairs = []
        for low in range(number, count - 1, 2):
            pairs += [(low, low + 1), (low + 1, low)]
        self.layers.append(lax.ppermute(self.edges[number], "slab", pairs))

    def take_layers(self, token):
        layers = ordered(self.layers, token)
        odd = bit_of(lax.axis_index("slab"), 0) == 1
        below, above = jnp.where(odd, layers[0], layers[1]), jnp.where(odd, layers[1], layers[0])
        rows = self.cells.shape[1]
        cells = jnp.concatenate([below[:, :rows], self.cells, above[:, :rows]], axis=0)
        before = jnp.concatenate([below[:, rows : rows + 1], self.before, above[:, rows : rows + 1]], axis=0)
        after = jnp.concatenate([below[:, rows + 1 :], self.after, above[:, rows + 1 :]], axis=0)
        padded = jnp.concatenate([before, cells, after], axis=1)
        self.cells = sweep_once(pad_x(padded), self.sources, self.absorption)
        return layers[0]


def stiffness(padded):
    along_x = padded[:, :, :-2] + padded[:, :, 2:]
    middle = padded[:, :, 1:-1]
    plus_mid = along_x + middle
    plane_sum = plus_mid[:, :-2] + plus_mid[:, 1:-1] + plus_mid[:, 2:]
    total_sum = plane_sum[:-2] + plane_sum[1:-1] + plane_sum[2:]
    cross_xy = along_x[:, :-2] + along_x[:, 2:]
    corner_sum = cross_xy[:-2] + cross_xy[2:]
    face_sum = (
        along_x[1:-1, 1:-1]
        + middle[1:-1, :-2]
        + middle[1:-1, 2:]
        + middle[:-2, 1:-1]
        + middle[2:, 1:-1]
    )
    center = middle[1:-1, 1:-1]
    edge_sum = total_sum - center - face_sum - corner_sum
    return center_weight * center - edge_sum / 6.0 - corner_sum / 12.0


def sweep_once(padded, sources, absorption):
    center = padded[1:-1, 1:-1, 1:-1]
    applied = stiffness(padded) + absorption * center
    return center + omega * (sources - applied) / (center_weight + absorption)


def pad_x(values):
    return jnp.pad(values, ((0, 0), (0, 0), (1, 1)))


def per_device(interior, sources, absorption, bem_panel, incident, node_cell, offset):
    slab_count = lax.axis_size("slab")
    blk_count = lax.axis_size("blk")
    slab_cols, width = incident.shape
    panel_rows = bem_panel.shape[0]
    node_total = slab_cols * slab_count
    chunk_rows = panel_rows // slab_count
    bits = slab_count.bit_length() - 1

    if blk_count == 2:
        other = lax.ppermute(interior, "blk", [(0, 1), (1, 0)])
        interiors = [interior, other]
    else:
        other = None
        gathered = lax.all_gather(interior, "blk", axis=0)
        interiors = [gathered[i] for i in range(blk_count)]

    units, first, done = chunk_rows // ROW_UNIT, 0, 0
    spans = []
    for share, order in PIECES:
        done += share
        last = (units * done // 16) * ROW_UNIT
        if last > first:
            if bits != len(order):
                order = [(bit + len(spans)) % bits for bit in range(bits)]
            spans.append((first, last - first, order))
        first = last
    carrier = min(CARRIER, len(spans) - 1)
    pieces = [
        Piece(at, rows, order, TILE if number == carrier else 0)
        for number, (at, rows, order) in enumerate(spans)
    ]
    cells = node_cell.reshape(slab_cols // LANES, LANES)

    panel = bem_panel.reshape((2,) * bits + (chunk_rows, slab_cols))
    inside = Interior(interior, other, sources, absorption)
    inside.make_layers(offset, first_layers)
    inside.send_layer(0)
    inside.send_layer(1)
    fields, squares, *far = first_products(
        [(piece, 0) for piece in pieces[:EARLY]], offset, interiors, cells, incident, panel
    )
    courses = [Course(piece, number, sent) for number, (piece, sent) in enumerate(zip(pieces, far))]
    token = far[0]
    events = EVENTS
    if len(pieces) * bits != sum(event.isdigit() for event in EVENTS):
        events = "F" * (len(pieces) - EARLY) + "Nabdc" + "".join(str(number) for number in range(len(pieces))) * bits
    for number_of_event, event in enumerate(events):
        if number_of_event == len(events) - 1:
            token = inside.cells
        if event == "F":
            number = len(courses)
            token = later_products([(pieces[number], 0)], offset, fields, squares, panel, token)[0]
            courses.append(Course(pieces[number], number, token))
        elif event == "N":
            near = later_products([(piece, 1) for piece in pieces], offset, fields, squares, panel, token)
            token = near[0]
        elif event == "a":
            token = inside.take_layers(token)
            inside.send_rows()
        elif event == "b":
            inside.take_rows(*ordered(inside.rows, token))
            token = inside.make_layers(token)
            inside.send_layer(0)
        elif event == "d":
            inside.layers = list(ordered(inside.layers, token))
            inside.edges = ordered(inside.edges, inside.layers[0])
            inside.send_layer(1)
            token = inside.edges[0]
        elif event == "c":
            token = inside.take_layers(token)
        elif event.isdigit() and courses[int(event)].done is None:
            token = courses[int(event)].arrive(near[int(event)], token)
    owned = pl.pallas_call(
        functools.partial(finish_kernel, node_total, carrier, [piece.rows for piece in pieces]),
        in_specs=[IN_VMEM] * len(pieces),
        out_specs=IN_VMEM,
        out_shape=jax.ShapeDtypeStruct((chunk_rows, width), jnp.float32),
        compiler_params=PARAMS,
        cost_estimate=COST,
        name="divide_by_norms",
    )(*[course.done for course in courses])

    return (inside.cells, owned)


def solution(mesh):
    in_specs = (
        P("slab", "blk", None),
        P("slab", "blk", None),
        P("slab", "blk", None),
        P("blk", "slab"),
        P("slab", None),
        P("slab"),
        P(),
    )
    out_specs = (P("slab", "blk", None), P(("blk", "slab"), None))
    return jax.shard_map(
        per_device, mesh=mesh, in_specs=in_specs, out_specs=out_specs, check_vma=False
    )
```
